128 devices in a mesh: rows: 8 (over x_lo, y), cols: 16 (over z, x_hi, core).
Axes of the slice: x: 4 (x_hi: 2, x_lo: 2; x = x_hi * 2 + x_lo), y: 4, z: 4, core: 2. Of those that a mesh axis runs over, the one named last changes fastest.
Arguments:
- snapshots: float32 [32768, 2048], P('rows', 'cols'), may hold values from -6 to 6
Outputs:
- rotated: float32 [32768, 2048], P('rows', 'cols')
The draws below stay inside these ranges and needn't reach their ends.
All inputs are finite; a program needn't handle non-finite values.
Results may differ from the reference program's by a relative error of at most 0.0003.
Values sent between devices are 32-bit elements; how exact they have to be, the bound alone decides.
No kernel may reach another device: no remote copies, remote signals or barrier semaphores. Data moves between devices by JAX's collectives and lax.ppermute only.
A program may use at most 64 MiB of HBM per device.

```python
import jax
import jax.numpy as jnp
from jax import lax

BLK = 64
NS_STEPS = 12
ROWS = 32768
BLOCKS = 32
COLUMNS = 2048
ROUNDS = 15


def draw_snapshots(key, part):
    key = jax.random.fold_in(key, 7)
    first = jax.random.fold_in(key, 0)
    values = jax.random.normal(first, (ROWS, COLUMNS), jnp.float32)
    return jnp.clip(values, -6.0, 6.0).astype(jnp.float32)


def setup_inputs(seed: int = 0) -> dict:
    streams_of = jax.random.split(jax.random.key(seed), 2)
    return {
        "snapshots": draw_snapshots(jax.random.fold_in(streams_of[1], 71), 0),
    }


def lowdin(gram):
    size = gram.shape[0]
    diag = jnp.diagonal(gram)
    scale = 1.0 / jnp.sqrt(diag)
    unit = gram * scale[:, None] * scale[None, :]
    eye = jnp.eye(size, dtype=jnp.float32)
    ymat = unit
    zmat = eye
    for step in range(NS_STEPS):
        middle = 1.5 * eye - 0.5 * jnp.dot(zmat, ymat, precision=lax.Precision.HIGHEST)
        ymat = jnp.dot(ymat, middle, precision=lax.Precision.HIGHEST)
        zmat = jnp.dot(middle, zmat, precision=lax.Precision.HIGHEST)
    return scale[:, None] * zmat / scale[None, :]

def reference(snapshots):
    count = BLOCKS // 2
    blocks = snapshots.reshape(ROWS, count, 2, BLK)
    tops = blocks[:, :, 0, :]
    bottoms = blocks[:, :, 1, :]
    for step in range(ROUNDS):
        pairs = jnp.concatenate([tops, bottoms], axis=2)
        grams = jnp.einsum('mpi,mpj->pij', pairs, pairs, precision=lax.Precision.HIGHEST)
        weights = jax.vmap(lowdin)(grams)
        pairs = jnp.einsum('mpi,pij->mpj', pairs, weights, precision=lax.Precision.HIGHEST)
        tops = pairs[:, :, :BLK]
        bottoms = pairs[:, :, BLK:]
        if step + 1 < ROUNDS:
            bottoms = jnp.roll(bottoms, 1, axis=1)
    bottoms = jnp.roll(bottoms, -(ROUNDS - 1), axis=1)
    return jnp.stack([tops, bottoms], axis=2).reshape(ROWS, COLUMNS)
```

```python
import functools

import jax
import jax.numpy as jnp
from jax import lax
from jax.experimental import pallas as pl
from jax.experimental.pallas import tpu as pltpu
from jax.sharding import PartitionSpec as P

NS_STEPS = 12
F32 = jnp.float32
BF16 = jnp.bfloat16


def halves(x):
    hi = x.astype(BF16)
    lo = (x - hi.astype(F32)).astype(BF16)
    return hi, lo


def thirds(x):
    hi = x.astype(BF16)
    rest = x - hi.astype(F32)
    mid = rest.astype(BF16)
    lo = (rest - mid.astype(F32)).astype(BF16)
    return hi, mid, lo


def beside(*parts):
    return jnp.concatenate(parts, axis=1)


def above(*parts):
    return jnp.concatenate(parts, axis=0)


def mm(a, b):
    return jnp.dot(a, b, preferred_element_type=F32)


def tdot(a, b):
    return lax.dot_general(a, b, (((0,), (0,)), ((), ())), preferred_element_type=F32)


def product(a, b):
    ah, am, al = a
    bh, bm, bl = b
    n = bh.shape[1]
    top = beside(bh, bm)
    one = mm(beside(ah, am), above(top, top))
    two = mm(beside(ah, al), above(bl, bh))
    return one[:, :n] + (one[:, n:] + two)


def eye_of(n):
    i = lax.broadcasted_iota(jnp.int32, (n, n), 0)
    j = lax.broadcasted_iota(jnp.int32, (n, n), 1)
    return (i == j).astype(F32)


def lowdin(gram):
    n = gram.shape[0]
    eye = eye_of(n)
    diag = gram * eye
    down = 1.0 / jnp.sqrt(jnp.sum(diag, axis=1, keepdims=True))
    across = 1.0 / jnp.sqrt(jnp.sum(diag, axis=0, keepdims=True))
    y = gram * down * across
    z = eye
    for step in range(NS_STEPS):
        ys, zs = thirds(y), thirds(z)
        m = 1.5 * eye - 0.5 * product(zs, ys)
        ms = thirds(m)
        y = product(ys, ms)
        z = product(ms, zs)
    return down * z / across


def gram_kernel(top_ref, bottom_ref, out_ref):
    w = top_ref.shape[1] // 2
    th, tl = halves(top_ref[...])
    bh, bl = halves(bottom_ref[...])
    hi, lo = beside(th, bh), beside(tl, bl)
    full = (tdot(hi, hi) + tdot(lo, lo)) + (tdot(hi, lo) + tdot(lo, hi))

    def fold(i, j):
        i, j = i * 2 * w, j * 2 * w
        return full[i : i + w, j : j + w] + full[i + w : i + 2 * w, j + w : j + 2 * w]

    out_ref[...] = above(beside(fold(0, 0), fold(0, 1)), beside(fold(1, 0), fold(1, 1)))


def rotate_kernel(gram_ref, top_ref, bottom_ref, new_top_ref, new_bottom_ref):
    w = top_ref.shape[1] // 2
    weights = lowdin(gram_ref[...])
    zero = jnp.zeros((w, w), F32)

    def twice(block):
        return above(beside(block, zero), beside(zero, block))

    wide = above(
        beside(twice(weights[:w, :w]), twice(weights[:w, w:])),
        beside(twice(weights[w:, :w]), twice(weights[w:, w:])),
    )
    wh, wl = halves(wide)
    rows = top_ref.shape[0]
    chunk = 512
    for i in range(rows // chunk):
        at = pl.ds(i * chunk, chunk)
        ph, plo = halves(beside(top_ref[at, :], bottom_ref[at, :]))
        fresh = mm(ph, wh) + (mm(ph, wl) + mm(plo, wh))
        new_top_ref[at, :] = fresh[:, : 2 * w]
        new_bottom_ref[at, :] = fresh[:, 2 * w :]


VMEM = pl.BlockSpec(memory_space=pltpu.VMEM)
PARAMS = pltpu.CompilerParams(vmem_limit_bytes=32 * 1024 * 1024)


def gram_of(top, bottom):
    n = top.shape[1]
    return pl.pallas_call(
        gram_kernel,
        out_shape=jax.ShapeDtypeStruct((n, n), F32),
        in_specs=[VMEM] * 2,
        out_specs=VMEM,
        compiler_params=PARAMS,
    )(top, bottom)


def rotate(gram, top, bottom):
    return pl.pallas_call(
        rotate_kernel,
        out_shape=[jax.ShapeDtypeStruct(top.shape, F32)] * 2,
        in_specs=[VMEM] * 3,
        out_specs=[VMEM] * 2,
        compiler_params=PARAMS,
    )(gram, top, bottom)


def shifted(block, axis, distance):
    n = lax.axis_size(axis)
    return lax.ppermute(block, axis, [((i - distance) % n, i) for i in range(n)])


def row_sum(part):
    n = lax.axis_size("rows")
    inner = 4
    total = part
    for d in range(1, inner):
        route = [(i, i - i % inner + (i + d) % inner) for i in range(n)]
        total = total + lax.ppermute(part, "rows", route)
    return total + lax.ppermute(total, "rows", [(i, (i + inner) % n) for i in range(n)])


def packed(block):
    half = block.shape[0] // 2
    return jnp.concatenate([block[:half], block[half:]], axis=1)


def unpacked(block):
    half = block.shape[1] // 2
    return jnp.concatenate([block[:, :half], block[:, half:]], axis=0)


def on_device(snapshots):
    width = snapshots.shape[1] // 2
    top = packed(snapshots[:, :width])
    bottom = packed(snapshots[:, width:])
    rounds = lax.axis_size("cols") - 1
    for r in range(rounds):
        gram = row_sum(gram_of(top, bottom))
        top, bottom = rotate(gram, top, bottom)
        bottom = shifted(bottom, "cols", 1 if r + 1 < rounds else 2)
    return jnp.concatenate([unpacked(top), unpacked(bottom)], axis=1)


def solution(mesh):
    return jax.shard_map(
        on_device, mesh=mesh, in_specs=(P("rows", "cols"),), out_specs=P("rows", "cols"), check_vma=False
    )
```

```python
import jax
import jax.numpy as jnp
from jax import lax
from jax.experimental import pallas as pl
from jax.experimental.pallas import tpu as pltpu
from jax.sharding import PartitionSpec as P

NS_STEPS = 12
BLK = 64
CHUNK = 512
F32 = jnp.float32
BF16 = jnp.bfloat16

FIRST = (((0, 2), (1, 3)), ((1, 2),))
MIDDLE = (((0, 3),), ((0, 2), (1, 3)), ((1, 2),))
LAST = (((0, 3),), ((0, 2), (1, 3)))


def halves(x):
    hi = x.astype(BF16)
    lo = (x - hi.astype(F32)).astype(BF16)
    return hi, lo


def beside(*parts):
    return jnp.concatenate(parts, axis=1)


def above(*parts):
    return jnp.concatenate(parts, axis=0)


def mm(a, b):
    return jnp.dot(a, b, preferred_element_type=F32)


def tdot(a, b):
    return lax.dot_general(a, b, (((0,), (0,)), ((), ())), preferred_element_type=F32)


def product(a, b):
    ah, al = a
    bh, bl = b
    n = bh.shape[1]
    row = beside(bh, bl)
    wide = mm(beside(ah, al), above(row, row))
    return wide[:, :n] + wide[:, n:]


def eye_of(n):
    i = lax.broadcasted_iota(jnp.int32, (n, n), 0)
    j = lax.broadcasted_iota(jnp.int32, (n, n), 1)
    return (i == j).astype(F32)


def lowdin(grams):
    eye = eye_of(2 * BLK)
    many = range(len(grams))
    down = [jnp.sqrt(jnp.sum(g * eye, axis=1, keepdims=True)) for g in grams]
    across = [jnp.sqrt(jnp.sum(g * eye, axis=0, keepdims=True)) for g in grams]
    e = [eye - grams[k] * (1.0 / down[k]) * (1.0 / across[k]) for k in many]
    z = [eye for k in many]
    for step in range(NS_STEPS):
        es = [halves(e[k]) for k in many]
        square = [product(es[k], es[k]) for k in many]
        z = [z[k] + 0.5 * (product(halves(z[k]), es[k]) if step else e[k]) for k in many]
        e = [0.75 * square[k] + 0.25 * product(halves(square[k]), es[k]) for k in many]
    weights = [z[k] * (1.0 / down[k]) * across[k] for k in many]
    turned = [z[k] * down[k] * (1.0 / across[k]) for k in many]
    fresh = [(eye - e[k]) * down[k] * across[k] for k in many]
    return weights, turned, fresh


def corners(block):
    w = BLK
    return ((block[:w, :w], block[:w, w:]), (block[w:, :w], block[w:, w:]))


class Gram:
    def __init__(self, tops, middle, bottoms):
        self.blocks = {}
        self.put((0, 1), (0, 1), tops)
        self.put((0, 1), (2, 3), middle)
        self.put((2, 3), (2, 3), bottoms)

    def put(self, rows, columns, block):
        cells = corners(block)
        for i, row in enumerate(rows):
            for j, column in enumerate(columns):
                if row <= column:
                    self.blocks[row, column] = cells[i][j]
                elif rows != columns:
                    self.blocks[column, row] = cells[i][j].T

    def cell(self, i, j):
        return self.blocks[i, j] if i <= j else self.blocks[j, i].T

    def get(self, rows, columns):
        return above(*[beside(*[self.cell(i, j) for j in columns]) for i in rows])


def wave(gram, levels, update_last):
    w = BLK
    zero = jnp.zeros((w, w), F32)
    unit = eye_of(w)
    columns = [above(*[unit if i == j else zero for i in range(4)]) for j in range(4)]
    for n, level in enumerate(levels):
        weights, turned, fresh = lowdin([gram.get(p, p) for p in level])
        for k, (t, b) in enumerate(level):
            if n == 0:
                (tt, tb), (bt, bb) = corners(weights[k])
                columns[t] = above(*[{t: tt, b: bt}.get(i, zero) for i in range(4)])
                columns[b] = above(*[{t: tb, b: bb}.get(i, zero) for i in range(4)])
            else:
                both = product(halves(beside(columns[t], columns[b])), halves(weights[k]))
                columns[t], columns[b] = both[:, :w], both[:, w:]
        if n + 1 == len(levels) and not update_last:
            break
        p = level[0]
        q = level[1] if len(level) > 1 else (1 - p[0], 5 - p[1])
        mixed = product(halves(turned[0]), halves(gram.get(p, q)))
        if len(level) > 1:
            mixed = product(halves(mixed), halves(weights[1]))
        gram.put(p, q, mixed)
        for k, pair in enumerate(level):
            gram.put(pair, pair, fresh[k])
    return beside(*columns)


def finish(gram, levels, urgent_ref, message_ref, tops_ref):
    w = 2 * BLK
    weights = wave(gram, levels, tops_ref is not None)
    message_ref[...] = weights[:, :w]
    urgent_ref[: 2 * w, :] = weights[:, w:]
    if tops_ref is not None:
        urgent_ref[2 * w :, :] = gram.get((2, 3), (2, 3))
        tops_ref[...] = gram.get((0, 1), (0, 1))


def first_wave_kernel(near_ref, far_ref, *outs):
    w = 2 * BLK
    sums = near_ref[...] + far_ref[...]
    finish(Gram(sums[:w, :], sums[w : 2 * w, :], sums[2 * w :, :]), FIRST, *outs)


def held_gram(near_ref, far_ref, old_tops_ref, old_urgent_ref):
    return Gram(old_tops_ref[...], near_ref[...] + far_ref[...], old_urgent_ref[4 * BLK :, :])


def wave_kernel(near_ref, far_ref, old_tops_ref, old_urgent_ref, *outs):
    finish(held_gram(near_ref, far_ref, old_tops_ref, old_urgent_ref), MIDDLE, *outs)


def last_wave_kernel(near_ref, far_ref, old_tops_ref, old_urgent_ref, urgent_ref, message_ref):
    finish(held_gram(near_ref, far_ref, old_tops_ref, old_urgent_ref), LAST, urgent_ref, message_ref, None)


def rotated(pair, wide):
    ph, plo = halves(pair)
    wh, wl = wide
    return mm(ph, wh) + (mm(ph, wl) + mm(plo, wh))


def cross(left, right):
    lh, ll = halves(left)
    rh, rl = halves(right)
    n = left.shape[1]
    wide = tdot(beside(lh, ll), beside(rh, rl))
    return (wide[:n, :n] + wide[n:, n:]) + (wide[:n, n:] + wide[n:, :n])


def chunks(ref):
    return [pl.ds(i * CHUNK, CHUNK) for i in range(ref.shape[0] // CHUNK)]


def first_gram_kernel(top_ref, bottom_ref, out_ref):
    w = 2 * BLK
    parts = None
    for at in chunks(top_ref):
        top, bottom = top_ref[at, :], bottom_ref[at, :]
        more = (cross(top, top), cross(top, bottom), cross(bottom, bottom))
        parts = more if parts is None else [a + b for a, b in zip(parts, more)]
    for i in range(3):
        out_ref[i * w : (i + 1) * w, :] = parts[i]


def side_kernel(weights_ref, top_ref, bottom_ref, out_ref):
    n = weights_ref.shape[0]
    wide = halves(weights_ref[n - 4 * BLK :, :])
    for at in chunks(top_ref):
        out_ref[at, :] = rotated(beside(top_ref[at, :], bottom_ref[at, :]), wide)


def bottom_kernel(weights_ref, message_ref, left_ref, bottom_ref, top_ref, new_bottom_ref, part_ref):
    wide = halves(weights_ref[: 4 * BLK, :])
    new_bottom_ref[top_ref.shape[0] :, :] = message_ref[...]
    part = None
    for at in chunks(top_ref):
        fresh = rotated(beside(left_ref[at, :], bottom_ref[at, :]), wide)
        new_bottom_ref[at, :] = fresh
        more = cross(top_ref[at, :], fresh)
        part = more if part is None else part + more
    part_ref[...] = part


VMEM = pl.BlockSpec(memory_space=pltpu.VMEM)
PARAMS = pltpu.CompilerParams(vmem_limit_bytes=32 * 1024 * 1024)


def call(kernel, shapes, *operands):
    out = pl.pallas_call(
        kernel,
        out_shape=[jax.ShapeDtypeStruct(s, F32) for s in shapes],
        in_specs=[VMEM] * len(operands),
        out_specs=[VMEM] * len(shapes),
        compiler_params=PARAMS,
    )(*operands)
    return out[0] if len(shapes) == 1 else out


def to_next_chip(block):
    n = lax.axis_size("cols")
    return lax.ppermute(block, "cols", [((i - 2) % n, i) for i in range(n)])


def hop(message):
    m, n = lax.axis_size("rows"), lax.axis_size("cols")
    route = [((i + m // 2) % m * n + (j - 2) % n, i * n + j) for i in range(m) for j in range(n)]
    return lax.ppermute(message, ("rows", "cols"), route)


def core_swap(block):
    n = lax.axis_size("cols")
    return lax.ppermute(block, "cols", [(i ^ 1, i) for i in range(n)])


def y_sum(part):
    n = lax.axis_size("rows")
    inner = n // 2
    terms = [part]
    for d in range(1, inner):
        route = [(i, i - i % inner + (i + d) % inner) for i in range(n)]
        terms.append(lax.ppermute(part, "rows", route))
    while len(terms) > 2:
        terms = [terms[0] + terms[1], *terms[2:]]
    return terms


def x_sum(part):
    n = lax.axis_size("rows")
    return [part, lax.ppermute(part, "rows", [(i, (i + n // 2) % n) for i in range(n)])]


def on_device(snapshots):
    w = BLK
    chips = lax.axis_size("cols") // 2
    core = lax.axis_index("cols") % 2
    rows = snapshots.shape[0] // 2
    own = lax.dynamic_slice(snapshots, (core * rows, 0), (rows, 2 * w))
    other = core_swap(lax.dynamic_slice(snapshots, ((1 - core) * rows, 0), (rows, 2 * w)))
    even, odd = jnp.where(core == 0, own, other), jnp.where(core == 0, other, own)
    top = jnp.concatenate([even[:, :w], odd[:, :w]], axis=1)
    bottom = jnp.concatenate([even[:, w:], odd[:, w:]], axis=1)

    block, small = top.shape, (2 * w, 2 * w)
    tall, taller, longer = (4 * w, 2 * w), (6 * w, 2 * w), (rows + 4 * w, 2 * w)
    part = call(first_gram_kernel, [taller], top, bottom)
    part = sum(x_sum(part + core_swap(part)))
    part, top, bottom = lax.optimization_barrier((part, top, bottom))
    left, left_bottom = to_next_chip(top), to_next_chip(bottom)
    sums = y_sum(part)
    for r in range(chips):
        if r == 0:
            urgent, message, tops = call(first_wave_kernel, [taller, tall, small], *sums)
        elif r + 1 < chips:
            urgent, message, tops = call(wave_kernel, [taller, tall, small], *sums, tops, first)
        else:
            urgent, message = call(last_wave_kernel, [tall, tall], *sums, tops, first)
        first = hop(urgent)
        top = call(side_kernel, [block], message, top, bottom)
        if r + 1 < chips:
            bottom, part = call(bottom_kernel, [longer, small], first, message, left, left_bottom, top)
            part = sum(x_sum(part + core_swap(part)))
            part, bottom = lax.optimization_barrier((part, bottom))
            soon = to_next_chip(bottom)
            sums = y_sum(part)
            left = call(side_kernel, [block], soon, left, left_bottom)
            left_bottom = soon
        else:
            bottom = call(side_kernel, [block], first, left, left_bottom)

    even = jnp.concatenate([top[:, :w], bottom[:, :w]], axis=1)
    odd = jnp.concatenate([top[:, w:], bottom[:, w:]], axis=1)
    own, other = jnp.where(core == 0, even, odd), core_swap(jnp.where(core == 0, odd, even))
    return jnp.concatenate([jnp.where(core == 0, own, other), jnp.where(core == 0, other, own)], axis=0)


def solution(mesh):
    return jax.shard_map(
        on_device, mesh=mesh, in_specs=(P("rows", "cols"),), out_specs=P("rows", "cols"), check_vma=False
    )
```

```python
import jax
import jax.numpy as jnp
from jax import lax
from jax.experimental import pallas as pl
from jax.experimental.pallas import tpu as pltpu
from jax.sharding import PartitionSpec as P

NS_STEPS = 12
BLK = 64
CHUNK = 2048
EARLY = 512
F32 = jnp.float32
BF16 = jnp.bfloat16

FIRST = (((0, 2), (1, 3)), ((1, 2),))
MIDDLE = (((0, 3),), ((0, 2), (1, 3)), ((1, 2),))
LAST = (((0, 3),), ((0, 2), (1, 3)))


def halves(x):
    hi = x.astype(BF16)
    lo = (x - hi.astype(F32)).astype(BF16)
    return hi, lo


def beside(*parts):
    return jnp.concatenate(parts, axis=1)


def above(*parts):
    return jnp.concatenate(parts, axis=0)


def mm(a, b):
    return jnp.dot(a, b, preferred_element_type=F32)


def tdot(a, b):
    return lax.dot_general(a, b, (((0,), (0,)), ((), ())), preferred_element_type=F32)


def product(a, b):
    ah, al = a
    bh, bl = b
    n = bh.shape[1]
    row = beside(bh, bl)
    wide = mm(beside(ah, al), above(row, row))
    return wide[:, :n] + wide[:, n:]


def fine_product(a, b):
    ah, al = halves(a)
    al_rest = (a - ah.astype(F32) - al.astype(F32)).astype(BF16)
    bh, bl = halves(b)
    bl_rest = (b - bh.astype(F32) - bl.astype(F32)).astype(BF16)
    return product((ah, al), (bh, bl)) + mm(beside(ah, al_rest), above(bl_rest, bh))


def eye_of(n):
    i = lax.broadcasted_iota(jnp.int32, (n, n), 0)
    j = lax.broadcasted_iota(jnp.int32, (n, n), 1)
    return (i == j).astype(F32)


def lowdin(grams):
    eye = eye_of(2 * BLK)
    many = range(len(grams))
    down = [jnp.sqrt(jnp.sum(g * eye, axis=1, keepdims=True)) for g in grams]
    across = [jnp.sqrt(jnp.sum(g * eye, axis=0, keepdims=True)) for g in grams]
    e = [eye - grams[k] * (1.0 / down[k]) * (1.0 / across[k]) for k in many]
    z = [eye for k in many]
    for step in range(NS_STEPS):
        es = [halves(e[k]) for k in many]
        square = [product(es[k], es[k]) for k in many]
        z = [z[k] + 0.5 * (product(halves(z[k]), es[k]) if step else e[k]) for k in many]
        e = [0.75 * square[k] + 0.25 * product(halves(square[k]), es[k]) for k in many]
    weights = [z[k] * (1.0 / down[k]) * across[k] for k in many]
    turned = [z[k] * down[k] * (1.0 / across[k]) for k in many]
    fresh = [(eye - e[k]) * down[k] * across[k] for k in many]
    return weights, turned, fresh


def corners(block):
    w = BLK
    return ((block[:w, :w], block[:w, w:]), (block[w:, :w], block[w:, w:]))


class Gram:
    def __init__(self, tops, middle, bottoms):
        self.blocks = {}
        self.put((0, 1), (0, 1), tops)
        self.put((0, 1), (2, 3), middle)
        self.put((2, 3), (2, 3), bottoms)

    def put(self, rows, columns, block):
        cells = corners(block)
        for i, row in enumerate(rows):
            for j, column in enumerate(columns):
                if row <= column:
                    self.blocks[row, column] = cells[i][j]
                elif rows != columns:
                    self.blocks[column, row] = cells[i][j].T

    def cell(self, i, j):
        return self.blocks[i, j] if i <= j else self.blocks[j, i].T

    def get(self, rows, columns):
        return above(*[beside(*[self.cell(i, j) for j in columns]) for i in rows])


def wave(gram, levels, update_last):
    w = BLK
    zero = jnp.zeros((w, w), F32)
    unit = eye_of(w)
    columns = [above(*[unit if i == j else zero for i in range(4)]) for j in range(4)]
    for n, level in enumerate(levels):
        weights, turned, fresh = lowdin([gram.get(p, p) for p in level])
        for k, (t, b) in enumerate(level):
            if n == 0:
                (tt, tb), (bt, bb) = corners(weights[k])
                columns[t] = above(*[{t: tt, b: bt}.get(i, zero) for i in range(4)])
                columns[b] = above(*[{t: tb, b: bb}.get(i, zero) for i in range(4)])
            else:
                both = product(halves(beside(columns[t], columns[b])), halves(weights[k]))
                columns[t], columns[b] = both[:, :w], both[:, w:]
        if n + 1 == len(levels) and not update_last:
            break
        p = level[0]
        q = level[1] if len(level) > 1 else (1 - p[0], 5 - p[1])
        mixed = product(halves(turned[0]), halves(gram.get(p, q)))
        if len(level) > 1:
            mixed = product(halves(mixed), halves(weights[1]))
        gram.put(p, q, mixed)
        for k, pair in enumerate(level):
            gram.put(pair, pair, fresh[k])
    return beside(*columns)


def this_core():
    return lax.axis_index("cols") % 2


def in_core_order(own, other):
    core = this_core()
    return jnp.where(core == 0, own, other), jnp.where(core == 0, other, own)


def finish(gram, levels, urgent_ref, message_ref, tops_ref):
    w = 2 * BLK
    weights = wave(gram, levels, tops_ref is not None)
    message_ref[...] = weights[:, :w]
    urgent_ref[: 2 * w, :] = weights[:, w:]
    if tops_ref is not None:
        urgent_ref[2 * w : 3 * w, :] = gram.get((2, 3), (2, 3))
        urgent_ref[3 * w :, :] = in_core_order(weights[:w, :w], weights[w:, :w])[0]
        tops_ref[...] = gram.get((0, 1), (0, 1))


def first_wave_kernel(near_ref, far_ref, *outs):
    w = 2 * BLK
    sums = near_ref[...] + far_ref[...]
    finish(Gram(sums[:w, :], sums[w : 2 * w, :], sums[2 * w :, :]), FIRST, *outs)


def held_gram(near_ref, far_ref, old_tops_ref, old_urgent_ref):
    w = 2 * BLK
    return Gram(old_tops_ref[...], near_ref[...] + far_ref[...], old_urgent_ref[2 * w : 3 * w, :])


def wave_kernel(near_ref, far_ref, old_tops_ref, old_urgent_ref, *outs):
    finish(held_gram(near_ref, far_ref, old_tops_ref, old_urgent_ref), MIDDLE, *outs)


def last_wave_kernel(near_ref, far_ref, old_tops_ref, old_urgent_ref, urgent_ref, message_ref):
    finish(held_gram(near_ref, far_ref, old_tops_ref, old_urgent_ref), LAST, urgent_ref, message_ref, None)


def weight_parts(weights):
    return beside(*halves(weights))


def rotated(pair, wide):
    hi, lo = halves(pair)
    n = wide.shape[1] // 2
    both = mm(hi, wide)
    return both[:, :n] + (both[:, n:] + mm(lo, wide[:, :n]))


def cross(left, right):
    lh, ll = halves(left)
    rh, rl = halves(right)
    n = left.shape[1]
    wide = tdot(beside(lh, ll), beside(rh, rl))
    return (wide[:n, :n] + wide[n:, n:]) + (wide[:n, n:] + wide[n:, :n])


def chunks(ref):
    return [pl.ds(i * CHUNK, CHUNK) for i in range(ref.shape[0] // CHUNK)]


def first_gram_kernel(top_ref, bottom_ref, out_ref):
    w = 2 * BLK
    parts = None
    for at in chunks(top_ref):
        top, bottom = top_ref[at, :], bottom_ref[at, :]
        more = (cross(top, top), cross(top, bottom), cross(bottom, bottom))
        parts = more if parts is None else [a + b for a, b in zip(parts, more)]
    for i in range(3):
        out_ref[i * w : (i + 1) * w, :] = parts[i]


def rotate_side(weights, top_ref, bottom_ref, out_ref):
    wide = weight_parts(weights)
    for at in chunks(top_ref):
        out_ref[at, :] = rotated(beside(top_ref[at, :], bottom_ref[at, :]), wide)


def top_kernel(weights_ref, top_ref, bottom_ref, out_ref):
    rotate_side(weights_ref[...], top_ref, bottom_ref, out_ref)


def left_kernel(urgent_ref, other_ref, left_ref, bottom_ref, out_ref):
    own = urgent_ref[6 * BLK :, :]
    rotate_side(above(*in_core_order(own, other_ref[...])), left_ref, bottom_ref, out_ref)


def bottom_kernel(urgent_ref, near_ref, far_ref, left_ref, bottom_ref, out_ref, part_ref):
    weights = urgent_ref[: 4 * BLK, :]
    part_ref[...] = fine_product(near_ref[...] + far_ref[...], weights)
    rotate_side(weights, left_ref, bottom_ref, out_ref)


def mixed_kernel(top_ref, left_ref, bottom_ref, part_ref):
    part = None
    for at in chunks(top_ref):
        top = top_ref[at, :]
        more = beside(cross(top, left_ref[at, :]), cross(top, bottom_ref[at, :]))
        part = more if part is None else part + more
    part_ref[...] = part


def last_kernel(weights_ref, left_ref, bottom_ref, top_ref, own_ref, other_ref):
    w = BLK
    wide = weight_parts(weights_ref[...])
    for at in chunks(top_ref):
        fresh = rotated(beside(left_ref[at, :], bottom_ref[at, :]), wide)
        top = top_ref[at, :]
        own, other = in_core_order(beside(top[:, :w], fresh[:, :w]), beside(top[:, w:], fresh[:, w:]))
        own_ref[at, :] = own
        other_ref[at, :] = other


def place_kernel(own_ref, other_ref, out_ref):
    rows = own_ref.shape[0]
    core = this_core()
    out_ref[pl.ds(pl.multiple_of(core * rows, rows), rows), :] = own_ref[...]
    out_ref[pl.ds(pl.multiple_of((1 - core) * rows, rows), rows), :] = other_ref[...]


VMEM = pl.BlockSpec(memory_space=pltpu.VMEM)
PARAMS = pltpu.CompilerParams(vmem_limit_bytes=32 * 1024 * 1024)


def call(kernel, shapes, *operands):
    out = pl.pallas_call(
        kernel,
        out_shape=[jax.ShapeDtypeStruct(s, F32) for s in shapes],
        in_specs=[VMEM] * len(operands),
        out_specs=[VMEM] * len(shapes),
        compiler_params=PARAMS,
    )(*operands)
    return out[0] if len(shapes) == 1 else out


def to_next_chip(block):
    n = lax.axis_size("cols")
    return lax.ppermute(block, "cols", [((i - 2) % n, i) for i in range(n)])


def hop(message):
    m, n = lax.axis_size("rows"), lax.axis_size("cols")
    route = [((i + m // 2) % m * n + (j - 2) % n, i * n + j) for i in range(m) for j in range(n)]
    return lax.ppermute(message, ("rows", "cols"), route)


def core_swap(block):
    n = lax.axis_size("cols")
    return lax.ppermute(block, "cols", [(i ^ 1, i) for i in range(n)])


def y_sum(part):
    n = lax.axis_size("rows")
    inner = n // 2
    terms = [part]
    for d in range(1, inner):
        route = [(i, i - i % inner + (i + d) % inner) for i in range(n)]
        terms.append(lax.ppermute(part, "rows", route))
    while len(terms) > 2:
        terms = [terms[0] + terms[1], *terms[2:]]
    return terms


def x_sum(part):
    n = lax.axis_size("rows")
    return [part, lax.ppermute(part, "rows", [(i, (i + n // 2) % n) for i in range(n)])]


def blocks_of(own, other, core):
    w = BLK
    even, odd = jnp.where(core == 0, own, other), jnp.where(core == 0, other, own)
    return tuple(jnp.concatenate([even[:, at], odd[:, at]], axis=1) for at in (slice(None, w), slice(w, None)))


def on_device(snapshots):
    w = BLK
    chips = lax.axis_size("cols") // 2
    core = lax.axis_index("cols") % 2
    rows = snapshots.shape[0] // 2
    own = lax.dynamic_slice(snapshots, (core * rows, 0), (rows, 2 * w))
    other = lax.dynamic_slice(snapshots, ((1 - core) * rows, 0), (rows, 2 * w))
    own, other = lax.optimization_barrier((own, other))
    next_early, other = to_next_chip(own[:EARLY]), core_swap(other)
    top, bottom = blocks_of(own, other, core)
    block, small = top.shape, (2 * w, 2 * w)
    tall, taller, long = (4 * w, 2 * w), (6 * w, 2 * w), (8 * w, 2 * w)

    part = call(first_gram_kernel, [taller], top, bottom)
    part = sum(x_sum(part + core_swap(part)))
    part, rest = lax.optimization_barrier((part, jnp.concatenate([own[EARLY:], other], axis=0)))
    next_rest = to_next_chip(rest)
    sums = y_sum(part)
    for r in range(chips):
        if r == 0:
            urgent, message, tops = call(first_wave_kernel, [long, tall, small], *sums)
            tops, next_early, next_rest = lax.optimization_barrier((tops, next_early, next_rest))
            next_own = jnp.concatenate([next_early, next_rest[: rows - EARLY]], axis=0)
            left, left_bottom = blocks_of(next_own, next_rest[rows - EARLY :], core)
        elif r + 1 < chips:
            urgent, message, tops = call(wave_kernel, [long, tall, small], *sums, tops, first)
        else:
            urgent, message = call(last_wave_kernel, [tall, tall], *sums, tops, first)
        first = hop(urgent)
        top = call(top_kernel, [block], message, top, bottom)
        if r + 1 < chips:
            sums = x_sum(call(mixed_kernel, [(2 * w, 4 * w)], top, left, left_bottom))
            bottom, part = call(bottom_kernel, [block, small], first, *sums, left, left_bottom)
            soon = to_next_chip(bottom)
            sums = y_sum(part + core_swap(part))
            left = call(left_kernel, [block], first, core_swap(first[6 * w :]), left, left_bottom)
            sums, left = lax.optimization_barrier((sums, left))
            left_bottom = soon
    own, other = call(last_kernel, [block, block], first, left, left_bottom, top)
    return call(place_kernel, [snapshots.shape], own, core_swap(other))


def solution(mesh):
    return jax.shard_map(
        on_device, mesh=mesh, in_specs=(P("rows", "cols"),), out_specs=P("rows", "cols"), check_vma=False
    )
```

```python
import jax
import jax.numpy as jnp
from jax import lax
from jax.experimental import pallas as pl
from jax.experimental.pallas import tpu as pltpu
from jax.sharding import PartitionSpec as P

NS_STEPS = 12
BLK = 64
CHUNK = 2048
EARLY = 512
F32 = jnp.float32
BF16 = jnp.bfloat16

FIRST = (((0, 2), (1, 3)), ((1, 2),))
MIDDLE = (((0, 3),), ((0, 2), (1, 3)), ((1, 2),))
LAST = (((0, 3),), ((0, 2), (1, 3)))


def halves(x):
    hi = x.astype(BF16)
    lo = (x - hi.astype(F32)).astype(BF16)
    return hi, lo


def beside(*parts):
    return jnp.concatenate(parts, axis=1)


def above(*parts):
    return jnp.concatenate(parts, axis=0)


def mm(a, b):
    return jnp.dot(a, b, preferred_element_type=F32)


def tdot(a, b):
    return lax.dot_general(a, b, (((0,), (0,)), ((), ())), preferred_element_type=F32)


def product(a, b):
    ah, al = a
    bh, bl = b
    n = bh.shape[1]
    row = beside(bh, bl)
    wide = mm(beside(ah, al), above(row, row))
    return wide[:, :n] + wide[:, n:]


def fine_product(a, b):
    ah, al = halves(a)
    al_rest = (a - ah.astype(F32) - al.astype(F32)).astype(BF16)
    bh, bl = halves(b)
    bl_rest = (b - bh.astype(F32) - bl.astype(F32)).astype(BF16)
    return product((ah, al), (bh, bl)) + mm(beside(ah, al_rest), above(bl_rest, bh))


def eye_of(n):
    i = lax.broadcasted_iota(jnp.int32, (n, n), 0)
    j = lax.broadcasted_iota(jnp.int32, (n, n), 1)
    return (i == j).astype(F32)


def lowdin(grams):
    eye = eye_of(2 * BLK)
    many = range(len(grams))
    down = [jnp.sqrt(jnp.sum(g * eye, axis=1, keepdims=True)) for g in grams]
    across = [jnp.sqrt(jnp.sum(g * eye, axis=0, keepdims=True)) for g in grams]
    e = [eye - grams[k] * (1.0 / down[k]) * (1.0 / across[k]) for k in many]
    z = [eye for k in many]
    for step in range(NS_STEPS):
        es = [halves(e[k]) for k in many]
        square = [product(es[k], es[k]) for k in many]
        z = [z[k] + 0.5 * (product(halves(z[k]), es[k]) if step else e[k]) for k in many]
        e = [0.75 * square[k] + 0.25 * product(halves(square[k]), es[k]) for k in many]
    weights = [z[k] * (1.0 / down[k]) * across[k] for k in many]
    turned = [z[k] * down[k] * (1.0 / across[k]) for k in many]
    fresh = [(eye - e[k]) * down[k] * across[k] for k in many]
    return weights, turned, fresh


def corners(block):
    w = BLK
    return ((block[:w, :w], block[:w, w:]), (block[w:, :w], block[w:, w:]))


class Gram:
    def __init__(self, tops, middle, bottoms):
        self.blocks = {}
        self.put((0, 1), (0, 1), tops)
        self.put((0, 1), (2, 3), middle)
        self.put((2, 3), (2, 3), bottoms)

    def put(self, rows, columns, block):
        cells = corners(block)
        for i, row in enumerate(rows):
            for j, column in enumerate(columns):
                if row <= column:
                    self.blocks[row, column] = cells[i][j]
                elif rows != columns:
                    self.blocks[column, row] = cells[i][j].T

    def cell(self, i, j):
        return self.blocks[i, j] if i <= j else self.blocks[j, i].T

    def get(self, rows, columns):
        return above(*[beside(*[self.cell(i, j) for j in columns]) for i in rows])


def wave(gram, levels, update_last):
    w = BLK
    zero = jnp.zeros((w, w), F32)
    unit = eye_of(w)
    columns = [above(*[unit if i == j else zero for i in range(4)]) for j in range(4)]
    for n, level in enumerate(levels):
        weights, turned, fresh = lowdin([gram.get(p, p) for p in level])
        for k, (t, b) in enumerate(level):
            if n == 0:
                (tt, tb), (bt, bb) = corners(weights[k])
                columns[t] = above(*[{t: tt, b: bt}.get(i, zero) for i in range(4)])
                columns[b] = above(*[{t: tb, b: bb}.get(i, zero) for i in range(4)])
            else:
                both = product(halves(beside(columns[t], columns[b])), halves(weights[k]))
                columns[t], columns[b] = both[:, :w], both[:, w:]
        if n + 1 == len(levels) and not update_last:
            break
        p = level[0]
        q = level[1] if len(level) > 1 else (1 - p[0], 5 - p[1])
        mixed = product(halves(turned[0]), halves(gram.get(p, q)))
        if len(level) > 1:
            mixed = product(halves(mixed), halves(weights[1]))
        gram.put(p, q, mixed)
        for k, pair in enumerate(level):
            gram.put(pair, pair, fresh[k])
    return beside(*columns)


def this_core():
    return lax.axis_index("cols") % 2


def in_core_order(own, other):
    core = this_core()
    return jnp.where(core == 0, own, other), jnp.where(core == 0, other, own)


def finish(gram, levels, urgent_ref, message_ref, tops_ref):
    w = 2 * BLK
    weights = wave(gram, levels, tops_ref is not None)
    message_ref[...] = weights[:, :w]
    urgent_ref[: 2 * w, :] = weights[:, w:]
    if tops_ref is not None:
        urgent_ref[2 * w : 3 * w, :] = gram.get((2, 3), (2, 3))
        urgent_ref[3 * w :, :] = in_core_order(weights[:w, :w], weights[w:, :w])[0]
        tops_ref[...] = gram.get((0, 1), (0, 1))


def first_wave_kernel(near_ref, far_ref, *outs):
    w = 2 * BLK
    sums = near_ref[...] + far_ref[...]
    finish(Gram(sums[:w, :], sums[w : 2 * w, :], sums[2 * w :, :]), FIRST, *outs)


def held_gram(near_ref, far_ref, old_tops_ref, old_urgent_ref):
    w = 2 * BLK
    return Gram(old_tops_ref[...], near_ref[...] + far_ref[...], old_urgent_ref[2 * w : 3 * w, :])


def wave_kernel(near_ref, far_ref, old_tops_ref, old_urgent_ref, *outs):
    finish(held_gram(near_ref, far_ref, old_tops_ref, old_urgent_ref), MIDDLE, *outs)


def last_wave_kernel(near_ref, far_ref, old_tops_ref, old_urgent_ref, urgent_ref, message_ref):
    finish(held_gram(near_ref, far_ref, old_tops_ref, old_urgent_ref), LAST, urgent_ref, message_ref, None)


def weight_parts(weights):
    return beside(*halves(weights))


def rotated(pair, wide):
    hi, lo = halves(pair)
    n = wide.shape[1] // 2
    both = mm(hi, wide)
    return both[:, :n] + (both[:, n:] + mm(lo, wide[:, :n]))


def cross(left, right):
    lh, ll = halves(left)
    rh, rl = halves(right)
    n = left.shape[1]
    wide = tdot(beside(lh, ll), beside(rh, rl))
    return (wide[:n, :n] + wide[n:, n:]) + (wide[:n, n:] + wide[n:, :n])


def chunks(ref):
    return [pl.ds(i * CHUNK, CHUNK) for i in range(ref.shape[0] // CHUNK)]


def first_gram_kernel(top_ref, bottom_ref, out_ref):
    w = 2 * BLK
    parts = None
    for at in chunks(top_ref):
        top, bottom = top_ref[at, :], bottom_ref[at, :]
        more = (cross(top, top), cross(top, bottom), cross(bottom, bottom))
        parts = more if parts is None else [a + b for a, b in zip(parts, more)]
    for i in range(3):
        out_ref[i * w : (i + 1) * w, :] = parts[i]


def rotate_side(weights, top_ref, bottom_ref, out_ref):
    wide = weight_parts(weights)
    for at in chunks(top_ref):
        out_ref[at, :] = rotated(beside(top_ref[at, :], bottom_ref[at, :]), wide)


def top_kernel(weights_ref, top_ref, bottom_ref, out_ref):
    rotate_side(weights_ref[...], top_ref, bottom_ref, out_ref)


def left_kernel(urgent_ref, other_ref, left_ref, bottom_ref, out_ref):
    own = urgent_ref[6 * BLK :, :]
    rotate_side(above(*in_core_order(own, other_ref[...])), left_ref, bottom_ref, out_ref)


def bottom_kernel(urgent_ref, near_ref, far_ref, left_ref, bottom_ref, out_ref, part_ref):
    weights = urgent_ref[: 4 * BLK, :]
    part_ref[...] = fine_product(near_ref[...] + far_ref[...], weights)
    rotate_side(weights, left_ref, bottom_ref, out_ref)


def mixed_kernel(top_ref, left_ref, bottom_ref, part_ref):
    part = None
    for at in chunks(top_ref):
        top = top_ref[at, :]
        more = beside(cross(top, left_ref[at, :]), cross(top, bottom_ref[at, :]))
        part = more if part is None else part + more
    part_ref[...] = part


def last_kernel(weights_ref, left_ref, bottom_ref, top_ref, own_ref, other_ref):
    w = BLK
    wide = weight_parts(weights_ref[...])
    for at in chunks(top_ref):
        fresh = rotated(beside(left_ref[at, :], bottom_ref[at, :]), wide)
        top = top_ref[at, :]
        own, other = in_core_order(beside(top[:, :w], fresh[:, :w]), beside(top[:, w:], fresh[:, w:]))
        own_ref[at, :] = own
        other_ref[at, :] = other


def place_kernel(own_ref, other_ref, out_ref):
    rows = own_ref.shape[0]
    core = this_core()
    out_ref[pl.ds(pl.multiple_of(core * rows, rows), rows), :] = own_ref[...]
    out_ref[pl.ds(pl.multiple_of((1 - core) * rows, rows), rows), :] = other_ref[...]


VMEM = pl.BlockSpec(memory_space=pltpu.VMEM)
PARAMS = pltpu.CompilerParams(vmem_limit_bytes=32 * 1024 * 1024)


def call(kernel, shapes, *operands):
    out = pl.pallas_call(
        kernel,
        out_shape=[jax.ShapeDtypeStruct(s, F32) for s in shapes],
        in_specs=[VMEM] * len(operands),
        out_specs=[VMEM] * len(shapes),
        compiler_params=PARAMS,
    )(*operands)
    return out[0] if len(shapes) == 1 else out


def to_next_chip(block):
    n = lax.axis_size("cols")
    return lax.ppermute(block, "cols", [((i - 2) % n, i) for i in range(n)])


def hop(message):
    m, n = lax.axis_size("rows"), lax.axis_size("cols")
    route = [((i + m // 2) % m * n + (j - 2) % n, i * n + j) for i in range(m) for j in range(n)]
    return lax.ppermute(message, ("rows", "cols"), route)


def core_swap(block):
    n = lax.axis_size("cols")
    return lax.ppermute(block, "cols", [(i ^ 1, i) for i in range(n)])


def y_sum(part):
    n = lax.axis_size("rows")
    inner = n // 2
    terms = [part]
    for d in range(1, inner):
        route = [(i, i - i % inner + (i + d) % inner) for i in range(n)]
        terms.append(lax.ppermute(part, "rows", route))
    while len(terms) > 2:
        terms = [terms[0] + terms[1], *terms[2:]]
    return terms


def x_sum(part):
    n = lax.axis_size("rows")
    return [part, lax.ppermute(part, "rows", [(i, (i + n // 2) % n) for i in range(n)])]


def blocks_of(own, other, core):
    w = BLK
    even, odd = jnp.where(core == 0, own, other), jnp.where(core == 0, other, own)
    return tuple(jnp.concatenate([even[:, at], odd[:, at]], axis=1) for at in (slice(None, w), slice(w, None)))


def on_device(snapshots):
    w = BLK
    chips = lax.axis_size("cols") // 2
    core = lax.axis_index("cols") % 2
    rows = snapshots.shape[0] // 2
    own = lax.dynamic_slice(snapshots, (core * rows, 0), (rows, 2 * w))
    other = lax.dynamic_slice(snapshots, ((1 - core) * rows, 0), (rows, 2 * w))
    own, other = lax.optimization_barrier((own, other))
    next_early, other = to_next_chip(own[:EARLY]), core_swap(other)
    top, bottom = blocks_of(own, other, core)
    block, small = top.shape, (2 * w, 2 * w)
    tall, taller, long = (4 * w, 2 * w), (6 * w, 2 * w), (8 * w, 2 * w)

    part = call(first_gram_kernel, [taller], top, bottom)
    part = sum(x_sum(part + core_swap(part)))
    part, rest = lax.optimization_barrier((part, jnp.concatenate([own[EARLY:], other], axis=0)))
    next_rest = to_next_chip(rest)
    sums = y_sum(part)
    for r in range(chips):
        if r == 0:
            urgent, message, tops = call(first_wave_kernel, [long, tall, small], *sums)
            tops, next_early, next_rest = lax.optimization_barrier((tops, next_early, next_rest))
            next_own = jnp.concatenate([next_early, next_rest[: rows - EARLY]], axis=0)
            left, left_bottom = blocks_of(next_own, next_rest[rows - EARLY :], core)
        elif r + 1 < chips:
            urgent, message, tops = call(wave_kernel, [long, tall, small], *sums, tops, first)
        else:
            urgent, message = call(last_wave_kernel, [tall, tall], *sums, tops, first)
        first = hop(urgent)
        top = call(top_kernel, [block], message, top, bottom)
        if r + 1 < chips:
            sums = x_sum(call(mixed_kernel, [(2 * w, 4 * w)], top, left, left_bottom))
            bottom, part = call(bottom_kernel, [block, small], first, *sums, left, left_bottom)
            soon = to_next_chip(bottom)
            sums = y_sum(part + core_swap(part))
            left = call(left_kernel, [block], first, core_swap(first[6 * w :]), left, left_bottom)
            if r + 2 < chips:
                sums, left = lax.optimization_barrier((sums, left))
            left_bottom = soon
    own, other = call(last_kernel, [block, block], first, left, left_bottom, top)
    return call(place_kernel, [snapshots.shape], own, core_swap(other))


def solution(mesh):
    return jax.shard_map(
        on_device, mesh=mesh, in_specs=(P("rows", "cols"),), out_specs=P("rows", "cols"), check_vma=False
    )
```
